256 devices in a mesh: head: 8 (over x_hi, y), blk: 32 (over x_lo, z, core).
Axes of the slice: x: 4 (x_hi: 2, x_lo: 2; x = x_hi * 2 + x_lo), y: 4, z: 8, core: 2. Of those that a mesh axis runs over, the one named last changes fastest.
Arguments:
- queries: bfloat16 [64, 128, 2048], P('blk', None, 'head'), may hold values from -8 to 8
- key_vectors: bfloat16 [64, 128, 2048], P('blk', None, 'head'), may hold values from -8 to 8
- value_vectors: bfloat16 [64, 128, 2048], P('blk', None, 'head'), may hold values from -6 to 6
- out_grad: bfloat16 [64, 128, 2048], P('blk', None, 'head'), may hold values from -6 to 6
- block_order: int32 [64], replicated, may hold values from 0 to 63, each once
Outputs:
- attended: bfloat16 [64, 128, 2048], P('blk')
- query_grad: bfloat16 [64, 128, 2048], P('blk', None, 'head')
- key_grad: bfloat16 [64, 128, 2048], P('blk', None, 'head')
- value_grad: bfloat16 [64, 128, 2048], P('blk', None, 'head')
The draws below stay inside these ranges and needn't reach their ends.
Inputs may be any that keep to these rules, and one draw needn't show every extreme that they name: `block_order`: a permutation of the 64 block numbers.
All inputs are finite; a program needn't handle non-finite values.
Results may differ from the reference program's by a relative error of at most 0.03.
Values may be sent and summed in bfloat16 or wider, within the bound.
A program may use at most 64 MiB of HBM per device.

```python
import jax
import jax.numpy as jnp
from jax import lax

HEADS = 16
DH = 128
SLOTS = 64
SPAN = 128
HD = 2048


def draw_queries(key, part):
    key = jax.random.fold_in(key, 1)
    shape = (SLOTS, SPAN, HEADS * DH)
    base = jnp.clip(1.6 * jax.random.normal(key, shape), -8.0, 8.0)
    return base.astype(jnp.bfloat16)


def draw_key_vectors(key, part):
    key = jax.random.fold_in(key, 2)
    shape = (SLOTS, SPAN, HEADS * DH)
    base = jnp.clip(1.6 * jax.random.normal(key, shape), -8.0, 8.0)
    return base.astype(jnp.bfloat16)


def level_of(own_key, shape, pieces, low, top_value):
    level, own = 1.0, jax.random.fold_in(own_key, 6)
    for axis_at, parts in pieces:
        heights = jnp.exp(jax.random.uniform(jax.random.fold_in(own, axis_at), (parts,), jnp.float32, low / len(pieces), top_value / len(pieces)))
        level = level * jnp.repeat(heights, shape[axis_at] // parts).reshape([-1 if axis == axis_at else 1 for axis in range(len(shape))])
    return level


def noise(stream_key, extent, scale, limit, split=(), held_as=jnp.bfloat16):
    entries = jax.random.normal(stream_key, extent, jnp.float32) * scale
    if len(split) > 0:
        entries = level_of(stream_key, extent, split, -0.22, 0.18) * entries
    return jnp.clip(entries, min=-limit, max=limit).astype(held_as)


def setup_inputs(seed: int = 0) -> dict:
    seeds = jax.random.split(jax.random.key(seed), 6)
    return {
        "queries": draw_queries(jax.random.fold_in(seeds[5], 71), 0),
        "key_vectors": draw_key_vectors(jax.random.fold_in(seeds[5], 71), 0),
        "value_vectors": noise(seeds[2], (SLOTS, SPAN, HD), 1.0, 6.0, ((0, 32), (2, 8))),
        "out_grad": noise(seeds[3], (SLOTS, SPAN, HD), 1.0, 6.0, ((0, 32), (2, 8))),
        "block_order": jax.random.permutation(seeds[4], SLOTS).astype(jnp.int32),
    }


def reference(queries, key_vectors, value_vectors, out_grad, block_order):
    seq_len = SLOTS * SPAN
    offsets = jnp.arange(SPAN, dtype=jnp.int32)
    positions = (block_order[:, None].astype(jnp.int32) * SPAN + offsets[None, :]).reshape(seq_len)
    visible = positions[None, :] <= positions[:, None]
    score_scale = DH ** -0.5

    def by_head(array):
        return jnp.transpose(array.reshape(seq_len, HEADS, DH), (1, 0, 2))

    def one_head(inputs):
        head_q, head_k, head_v, head_g = inputs
        scores = jnp.dot(head_q, head_k.T, preferred_element_type=jnp.float32) * score_scale
        scores = jnp.where(visible, scores, -jnp.inf)
        row_max = jnp.max(scores, axis=1, keepdims=True)
        log_total = row_max + jnp.log(jnp.sum(jnp.exp(scores - row_max), axis=1, keepdims=True))
        probs = jnp.exp(scores - log_total)
        probs_low = probs.astype(jnp.bfloat16)
        attended = jnp.dot(probs, head_v.astype(jnp.float32), preferred_element_type=jnp.float32, precision=lax.Precision.HIGHEST).astype(jnp.bfloat16)
        row_delta = jnp.sum(head_g.astype(jnp.float32) * attended.astype(jnp.float32), axis=1, keepdims=True)
        dprob = jnp.dot(head_g, head_v.T, preferred_element_type=jnp.float32)
        dscore = (probs * (dprob - row_delta) * score_scale).astype(jnp.bfloat16)
        query_grad = jnp.dot(dscore, head_k, preferred_element_type=jnp.float32).astype(jnp.bfloat16)
        key_grad = jnp.dot(dscore.T, head_q, preferred_element_type=jnp.float32).astype(jnp.bfloat16)
        value_grad = jnp.dot(probs_low.T, head_g, preferred_element_type=jnp.float32).astype(jnp.bfloat16)
        return attended, query_grad, key_grad, value_grad

    results = lax.map(one_head, (by_head(queries), by_head(key_vectors), by_head(value_vectors), by_head(out_grad)))

    def restore(array):
        return jnp.transpose(array, (1, 0, 2)).reshape(SLOTS, SPAN, HEADS * DH)

    return (restore(results[0]), restore(results[1]), restore(results[2]), restore(results[3]))
```

```python
import functools
import math

import jax
import jax.numpy as jnp
from jax import lax
from jax.experimental import pallas as pl
from jax.experimental.pallas import tpu as pltpu
from jax.sharding import PartitionSpec as P

MESH = pl.DeviceIdType.MESH
DH = 128
SPAN = 128
ROWS = 256
CHUNK = 512
WIDE = 2048
SCALE = DH**-0.5
SCALE2 = DH**-0.5 * math.log2(math.e)
LOW = -1e30
F32 = jnp.float32
BF16 = jnp.bfloat16
NN = (((1,), (0,)), ((), ()))
NT = (((1,), (1,)), ((), ()))
TK, TQ, TV, TG = 0, 1, 2, 3
RO, RV, RK, RQ = 0, 1, 2, 3


def dot(a, b, dims):
    return lax.dot_general(a, b, dims, preferred_element_type=F32)


def kernel(
    order, q_in, k_in, v_in, g_in,
    att_out, dq_out, dk_out, dv_out,
    gathered, probs, qpos, chunk_max, chunk_sum, stat_out, stat_in, delta_out, delta_in, factor,
    turned, key_total, value_held, out_held, query_held,
    staged, from_a_mid, from_a, from_b, from_own,
    g_send, g_recv, r_send, r_recv, s_send, s_recv, d_send, d_recv, h_send, h_recv,
):
    blk = lax.axis_index("blk")
    head = lax.axis_index("head")
    core = blk % 2
    z = (blk // 2) % 8
    x = blk // 16
    odd = z % 2
    other = 1 - core
    y = head % 4
    xh = head // 4

    def at(xx, zz):
        return xx * 16 + zz * 2

    zq = z + 1 - 2 * odd
    zka = (z + 2 * odd + 7) % 8
    zkb = (z + 11 - 6 * odd) % 8
    zkab = (zkb + 2 * (1 - odd) + 7) % 8
    q_a, q_b, q_ab = at(1 - x, z), at(x, zq), at(1 - x, zq)
    k_a, k_b = at(x, zka), at(x, zkb)
    own = at(x, z)
    near_a = {TK: k_a, TV: k_a, TQ: q_a, TG: q_a}
    near_b = {TK: k_b, TV: k_b, TQ: q_b, TG: q_b}
    inputs = {TK: k_in, TV: v_in, TQ: q_in, TG: g_in}

    barrier = pltpu.get_barrier_semaphore()
    chips = (q_a, q_b, q_ab, k_a, k_b)
    for chip in chips:
        for r in range(2):
            pl.semaphore_signal(barrier, inc=1, device_id={"blk": chip + r}, device_id_type=MESH)
    pl.semaphore_signal(barrier, inc=1, device_id={"blk": own + other}, device_id_type=MESH)
    heads_y = [xh * 4 + (y + n) % 4 for n in (1, 2, 3)]
    head_x = (1 - xh) * 4 + y
    for target in heads_y + [head_x]:
        pl.semaphore_signal(barrier, inc=1, device_id={"head": target}, device_id_type=MESH)
    pl.semaphore_wait(barrier, 2 * len(chips) + 1 + 4)

    started = []

    def remote(src, dst, send, recv, axis, device):
        copy = pltpu.make_async_remote_copy(
            src_ref=src, dst_ref=dst, send_sem=send, recv_sem=recv,
            device_id={axis: device}, device_id_type=MESH,
        )
        copy.start()
        started.append(copy)

    def lanes(h):
        return pl.ds(pl.multiple_of(h * DH, DH), DH)

    def rows(r):
        return pl.ds(pl.multiple_of(r * ROWS, ROWS), ROWS)

    def send_b(t):
        for h in range(2):
            remote(inputs[t].at[:, lanes(h)], gathered.at[t, 2, rows(core)],
                   g_send.at[t, h], g_recv.at[t, 4 + core], "blk", near_b[t] + h)

    def send_a(t):
        for h in range(2):
            remote(inputs[t].at[:, lanes(h)], gathered.at[t, 1, rows(core)],
                   g_send.at[t, 2 + h], g_recv.at[t, 2 + core], "blk", near_a[t] + h)

    local = {}

    def send_own(t):
        remote(inputs[t].at[:, lanes(other)], gathered.at[t, 0, rows(core)],
               g_send.at[t, 4], g_recv.at[t, 0], "blk", own + other)
        local[t] = pltpu.make_async_copy(
            inputs[t].at[:, lanes(core)], gathered.at[t, 0, rows(core)], g_recv.at[t, 1])
        local[t].start()

    def arrived(dst, sem):
        pltpu.make_async_remote_copy(
            src_ref=dst, dst_ref=dst, send_sem=sem, recv_sem=sem,
            device_id={"blk": own + other}, device_id_type=MESH,
        ).wait_recv()

    def wait_own(t):
        local[t].wait()
        arrived(gathered.at[t, 0, rows(other)], g_recv.at[t, 0])

    def wait_slot(t, slot):
        for r in range(2):
            arrived(gathered.at[t, slot, pl.ds(r * ROWS, ROWS)], g_recv.at[t, slot * 2 + r])

    def wait_forward(t):
        for r in range(2):
            piece = pl.ds(r * ROWS, ROWS)
            arrived(gathered.at[t, 2, piece], g_recv.at[t, 4 + r])
            remote(gathered.at[t, 2, piece], gathered.at[t, 3, piece],
                   g_send.at[t, 5 + r], g_recv.at[t, 6 + r], "blk", near_a[t] + core)

    for t in (TK, TQ):
        send_b(t)
    for t in (TK, TQ):
        send_own(t)
        send_a(t)
    for t in (TV, TG):
        send_b(t)
    for t in (TV, TG):
        send_a(t)
        send_own(t)

    lane = lax.broadcasted_iota(jnp.int32, (1, SPAN), 1)
    for s, (xx, zz) in enumerate(((x, z), (1 - x, z), (x, zq), (1 - x, zq))):
        for n in range(4):
            first = order[4 * (xx * 8 + zz) + n] * SPAN
            qpos[:, pl.ds(s * CHUNK + n * SPAN, SPAN)] = first + lane
    key_z = (z, zka, zkb, zkab)
    down = lax.broadcasted_iota(jnp.int32, (SPAN, CHUNK), 0)

    def cols(i):
        return pl.ds(i * CHUNK, CHUNK)

    def score_tile(j, i):
        s = dot(gathered[TK, j], gathered[TQ, i], NT)
        place = qpos[:, cols(i)]
        parts = []
        for n in range(4):
            first = order[4 * (x * 8 + key_z[j]) + n] * SPAN
            parts.append(jnp.where(down <= place - first, s[n * SPAN:(n + 1) * SPAN], LOW))
        s = jnp.concatenate(parts, axis=0)
        top = jnp.max(s, axis=0, keepdims=True)
        p = jnp.exp2((s - top) * SCALE2)
        chunk_sum[j:j + 1, cols(i)] = jnp.sum(p, axis=0, keepdims=True)
        chunk_max[j:j + 1, cols(i)] = top
        probs[j, :, cols(i)] = p.astype(BF16)

    wait_own(TK)
    wait_own(TQ)
    score_tile(0, 0)
    wait_slot(TQ, 1)
    score_tile(0, 1)
    wait_forward(TQ)
    score_tile(0, 2)
    wait_slot(TK, 1)
    score_tile(1, 0)
    score_tile(1, 1)
    wait_forward(TK)
    score_tile(1, 2)
    score_tile(2, 0)
    score_tile(2, 1)
    score_tile(2, 2)
    wait_slot(TQ, 3)
    score_tile(0, 3)
    score_tile(1, 3)
    score_tile(2, 3)
    wait_forward(TG)
    wait_slot(TK, 3)
    for i in range(4):
        score_tile(3, i)

    peers = (q_a, q_b, q_ab)
    tops = [chunk_max[j:j + 1, :] for j in range(4)]
    sums = [chunk_sum[j:j + 1, :] for j in range(4)]
    top = functools.reduce(jnp.maximum, tops)
    total = sum(s * jnp.exp2((m - top) * SCALE2) for s, m in zip(sums, tops))
    stat_out[0:1, :] = top
    stat_out[1:2, :] = total
    for n, peer in enumerate(peers):
        remote(stat_out, stat_in.at[n], s_send.at[n], s_recv.at[n], "blk", peer + core)
    wait_forward(TV)

    def turned_row(ref_row, n):
        return jnp.concatenate([ref_row[:, cols(s ^ (n + 1))] for s in range(4)], axis=1)

    wait_own(TV)
    wait_own(TG)
    wait_slot(TV, 1)
    wait_slot(TG, 1)
    all_tops, all_sums = [top], [total]
    for n in range(3):
        arrived(stat_in.at[n], s_recv.at[n])
        all_tops.append(turned_row(stat_in.at[n, pl.ds(0, 1)], n))
        all_sums.append(turned_row(stat_in.at[n, pl.ds(1, 1)], n))
    whole_top = functools.reduce(jnp.maximum, all_tops)
    whole_sum = sum(s * jnp.exp2((m - whole_top) * SCALE2) for s, m in zip(all_sums, all_tops))
    inverse = 1.0 / whole_sum
    for j in range(4):
        factor[j:j + 1, :] = jnp.exp2((tops[j] - whole_top) * SCALE2) * inverse

    def weigh(j, i):
        p = probs[j, :, cols(i)] * factor[j:j + 1, cols(i)].astype(BF16)
        probs[j, :, cols(i)] = p
        return dot(gathered[TV, j].T, p, NN)

    for i in range(4):
        turned[:, cols(i)] = weigh(0, i) + weigh(1, i) + weigh(2, i)
    wait_slot(TG, 3)
    wait_slot(TV, 3)

    red_a = {RO: q_a, RQ: q_a, RK: k_a, RV: k_a}
    red_b = {RO: q_b, RQ: q_b, RK: k_b, RV: k_b}

    def reduce_ab(t, part):
        staged[t, 3] = part.astype(BF16)
        remote(staged.at[t, 3], from_a_mid.at[t], r_send.at[t, 0], r_recv.at[t, 0], "blk", red_a[t] + core)

    def reduce_b(t, part):
        arrived(from_a_mid.at[t], r_recv.at[t, 0])
        staged[t, 2] = (part + from_a_mid[t].astype(F32)).astype(BF16)
        for r in range(2):
            remote(staged.at[t, 2, pl.ds(r * ROWS, ROWS)], from_b.at[t, core],
                   r_send.at[t, 1 + r], r_recv.at[t, 1 + core], "blk", red_b[t] + r)

    def reduce_a(t, part):
        staged[t, 1] = part.astype(BF16)
        for r in range(2):
            remote(staged.at[t, 1, pl.ds(r * ROWS, ROWS)], from_a.at[t, core],
                   r_send.at[t, 3 + r], r_recv.at[t, 3 + core], "blk", red_a[t] + r)

    def reduce_own(t, part):
        staged[t, 0] = part.astype(BF16)
        remote(staged.at[t, 0, rows(other)], from_own.at[t, core],
               r_send.at[t, 5], r_recv.at[t, 5], "blk", own + other)
        from_own[t, core] = staged[t, 0, rows(core)]

    def reduced(t):
        arrived(from_own.at[t, other], r_recv.at[t, 5])
        for h in range(2):
            arrived(from_a.at[t, h], r_recv.at[t, 3 + h])
            arrived(from_b.at[t, h], r_recv.at[t, 1 + h])
        return [
            (from_own[t, h].astype(F32) + from_a[t, h].astype(F32) + from_b[t, h].astype(F32)).astype(BF16)
            for h in range(2)
        ]

    for i in (3, 2, 1, 0):
        o = turned[:, cols(i)] + weigh(3, i)
        delta_out[:, cols(i)] = jnp.sum(o * gathered[TG, i].astype(F32).T, axis=0, keepdims=True)
        o = o.T
        if i == 3:
            reduce_ab(RO, o)
        elif i == 2:
            out_held[...] = o
        elif i == 1:
            reduce_a(RO, o)
        else:
            reduce_own(RO, o)
    for n, peer in enumerate(peers):
        remote(delta_out, delta_in.at[n], d_send.at[n], d_recv.at[n], "blk", peer + core)

    for j in (3, 2, 1, 0):
        part = sum(dot(probs[j, :, cols(i)], gathered[TG, i], NN) for i in range(4))
        if j == 3:
            reduce_ab(RV, part)
        elif j == 2:
            value_held[...] = part
        elif j == 1:
            reduce_a(RV, part)
        else:
            reduce_own(RV, part)

    delta = delta_out[...]
    for n in range(3):
        arrived(delta_in.at[n], d_recv.at[n])
        delta = delta + turned_row(delta_in.at[n], n)
    delta_out_rows = [delta[:, i * CHUNK:(i + 1) * CHUNK] for i in range(4)]

    fresh_k, fresh_q = set(), set()

    def grad_tile(j, i):
        dp = dot(gathered[TV, j], gathered[TG, i], NT)
        ds = (probs[j, :, cols(i)].astype(F32) * (dp - delta_out_rows[i])).astype(BF16)
        key_part = dot(ds, gathered[TQ, i], NN)
        query_part = dot(gathered[TK, j].T, ds, NN)
        if j in fresh_k:
            key_total[j] += key_part
        else:
            key_total[j] = key_part
        if i in fresh_q:
            turned[:, cols(i)] += query_part
        else:
            turned[:, cols(i)] = query_part
        fresh_k.add(j)
        fresh_q.add(i)

    def key_part_of(j):
        return key_total[j] * SCALE

    def query_part_of(i):
        return turned[:, cols(i)].T * SCALE

    for i in range(4):
        grad_tile(3, i)
    reduce_ab(RK, key_part_of(3))
    for j in range(3):
        grad_tile(j, 3)
    reduce_ab(RQ, query_part_of(3))
    reduce_b(RO, out_held[...])
    reduce_b(RV, value_held[...])
    for i in range(3):
        grad_tile(2, i)
    for j in range(2):
        grad_tile(j, 2)
    reduce_b(RK, key_part_of(2))
    reduce_b(RQ, query_part_of(2))
    for j in (1, 0):
        for i in (1, 0):
            grad_tile(j, i)
    reduce_a(RK, key_part_of(1))
    reduce_a(RQ, query_part_of(1))
    reduce_own(RK, key_part_of(0))
    reduce_own(RQ, query_part_of(0))

    def block_of(h):
        return pl.ds(pl.multiple_of(h * 2 * DH, 2 * DH), 2 * DH)

    mine = reduced(RO)
    att_out[:, block_of(head)] = jnp.concatenate(mine, axis=1)

    def share(source, base, targets):
        for n, target in enumerate(targets):
            remote(att_out.at[:, block_of(source)], att_out.at[:, block_of(source)],
                   h_send.at[base + n], h_recv.at[source], "head", target)

    def wait_share(source):
        arrived(att_out.at[:, block_of(source)], h_recv.at[source])

    share(head, 0, [head_x] + heads_y)

    value = reduced(RV)
    for h in range(2):
        dv_out[:, h * DH:(h + 1) * DH] = value[h]

    wait_share(head_x)
    share(head_x, 4, heads_y)

    for t, out in ((RK, dk_out), (RQ, dq_out)):
        part = reduced(t)
        for h in range(2):
            out[:, h * DH:(h + 1) * DH] = part[h]
    for n in (1, 2, 3):
        wait_share(xh * 4 + (y + n) % 4)
        wait_share((1 - xh) * 4 + (y + n) % 4)
    for copy in started:
        copy.wait_send()


def body(queries, key_vectors, value_vectors, out_grad, block_order):
    def flat(array):
        return array.reshape(ROWS, 2 * DH)

    vmem = pl.BlockSpec(memory_space=pltpu.VMEM)
    dma = pltpu.SemaphoreType.DMA
    small = jax.ShapeDtypeStruct((ROWS, 2 * DH), BF16)
    outs = pl.pallas_call(
        kernel,
        out_shape=(jax.ShapeDtypeStruct((ROWS, 16 * DH), BF16), small, small, small),
        in_specs=[pl.BlockSpec(memory_space=pltpu.SMEM)] + [vmem] * 4,
        out_specs=(vmem,) * 4,
        scratch_shapes=[
            pltpu.VMEM((4, 4, CHUNK, DH), BF16),
            pltpu.VMEM((4, CHUNK, WIDE), BF16),
            pltpu.VMEM((1, WIDE), jnp.int32),
            pltpu.VMEM((4, WIDE), F32),
            pltpu.VMEM((4, WIDE), F32),
            pltpu.VMEM((2, WIDE), F32),
            pltpu.VMEM((3, 2, WIDE), F32),
            pltpu.VMEM((1, WIDE), F32),
            pltpu.VMEM((3, 1, WIDE), F32),
            pltpu.VMEM((4, WIDE), F32),
            pltpu.VMEM((DH, WIDE), F32),
            pltpu.VMEM((4, CHUNK, DH), F32),
            pltpu.VMEM((CHUNK, DH), F32),
            pltpu.VMEM((CHUNK, DH), F32),
            pltpu.VMEM((CHUNK, DH), F32),
            pltpu.VMEM((4, 4, CHUNK, DH), BF16),
            pltpu.VMEM((4, CHUNK, DH), BF16),
            pltpu.VMEM((4, 2, ROWS, DH), BF16),
            pltpu.VMEM((4, 2, ROWS, DH), BF16),
            pltpu.VMEM((4, 2, ROWS, DH), BF16),
            dma((4, 7)), dma((4, 8)),
            dma((4, 6)), dma((4, 6)),
            dma((3,)), dma((3,)),
            dma((3,)), dma((3,)),
            dma((7,)), dma((8,)),
        ],
        compiler_params=pltpu.CompilerParams(
            collective_id=0, has_side_effects=True, vmem_limit_bytes=56 << 20
        ),
        cost_estimate=pl.CostEstimate(
            flops=12 * WIDE * WIDE * DH, bytes_accessed=3 << 20, transcendentals=WIDE * WIDE
        ),
    )(block_order, flat(queries), flat(key_vectors), flat(value_vectors), flat(out_grad))
    attended, query_grad, key_grad, value_grad = outs
    return (
        attended.reshape(2, SPAN, 16 * DH),
        query_grad.reshape(2, SPAN, 2 * DH),
        key_grad.reshape(2, SPAN, 2 * DH),
        value_grad.reshape(2, SPAN, 2 * DH),
    )


def solution(mesh):
    split = P("blk", None, "head")
    return jax.shard_map(
        body,
        mesh=mesh,
        in_specs=(split, split, split, split, P()),
        out_specs=(P("blk", None, None), split, split, split),
        check_vma=False,
    )
```

```python
import functools
import math

import jax
import jax.numpy as jnp
from jax import lax
from jax.experimental import pallas as pl
from jax.experimental.pallas import tpu as pltpu
from jax.sharding import PartitionSpec as P

MESH = pl.DeviceIdType.MESH
DH = 128
SPAN = 128
ROWS = 256
CHUNK = 512
WIDE = 2048
SCALE = DH**-0.5
SCALE2 = DH**-0.5 * math.log2(math.e)
LOW = -1e30
F32 = jnp.float32
BF16 = jnp.bfloat16
NN = (((1,), (0,)), ((), ()))
NT = (((1,), (1,)), ((), ()))
TK, TQ, TV, TG = 0, 1, 2, 3
RO, RV, RK, RQ = 0, 1, 2, 3


def dot(a, b, dims):
    return lax.dot_general(a, b, dims, preferred_element_type=F32)


def kernel(
    order, q_in, k_in, v_in, g_in,
    att_out, dq_out, dk_out, dv_out,
    gathered, probs, dprobs, qpos, chunk_max, chunk_sum, stat_out, stat_in, delta_out, delta_in, factor,
    turned, key_total, value_held, key_held, query_held,
    staged, from_a_mid, from_a, from_b, from_own, from_ab,
    g_send, g_recv, r_send, r_recv, s_send, s_recv, d_send, d_recv, h_send, h_recv,
):
    blk = lax.axis_index("blk")
    head = lax.axis_index("head")
    core = blk % 2
    z = (blk // 2) % 8
    x = blk // 16
    odd = z % 2
    other = 1 - core
    y = head % 4
    xh = head // 4

    def at(xx, zz):
        return xx * 16 + zz * 2

    zq = z + 1 - 2 * odd
    zka = (z + 2 * odd + 7) % 8
    zkb = (z + 11 - 6 * odd) % 8
    zkab = (zkb + 2 * (1 - odd) + 7) % 8
    q_a, q_b, q_ab = at(1 - x, z), at(x, zq), at(1 - x, zq)
    k_a, k_b = at(x, zka), at(x, zkb)
    own = at(x, z)
    near_a = {TK: k_a, TV: k_a, TQ: q_a, TG: q_a}
    near_b = {TK: k_b, TV: k_b, TQ: q_b, TG: q_b}
    inputs = {TK: k_in, TV: v_in, TQ: q_in, TG: g_in}

    barrier = pltpu.get_barrier_semaphore()
    chips = (q_a, q_b, q_ab, k_a, k_b)
    for chip in chips:
        for r in range(2):
            pl.semaphore_signal(barrier, inc=1, device_id={"blk": chip + r}, device_id_type=MESH)
    pl.semaphore_signal(barrier, inc=1, device_id={"blk": own + other}, device_id_type=MESH)
    heads_y = [xh * 4 + (y + n) % 4 for n in (1, 2, 3)]
    head_x = (1 - xh) * 4 + y
    for target in heads_y + [head_x]:
        pl.semaphore_signal(barrier, inc=1, device_id={"head": target}, device_id_type=MESH)

    def lanes(h):
        return pl.ds(pl.multiple_of(h * DH, DH), DH)

    def rows(r):
        return pl.ds(pl.multiple_of(r * ROWS, ROWS), ROWS)

    def cols(i):
        return pl.ds(i * CHUNK, CHUNK)

    halves = (pl.ds(0, ROWS), pl.ds(ROWS, ROWS))

    local = {}
    for t in (TK, TQ, TV, TG):
        local[t] = pltpu.make_async_copy(
            inputs[t].at[:, lanes(core)], gathered.at[t, 0, rows(core)], g_recv.at[t, 1])
        local[t].start()
    lane = lax.broadcasted_iota(jnp.int32, (1, SPAN), 1)
    for s, (xx, zz) in enumerate(((x, z), (1 - x, z), (x, zq), (1 - x, zq))):
        for n in range(4):
            first = order[4 * (xx * 8 + zz) + n] * SPAN
            qpos[:, pl.ds(s * CHUNK + n * SPAN, SPAN)] = first + lane
    pl.semaphore_wait(barrier, 2 * len(chips) + 1 + 4)

    started = []

    def remote(src, dst, send, recv, axis, device):
        copy = pltpu.make_async_remote_copy(
            src_ref=src, dst_ref=dst, send_sem=send, recv_sem=recv,
            device_id={axis: device}, device_id_type=MESH,
        )
        copy.start()
        started.append(copy)

    PIECES = 2
    PIECE = ROWS // PIECES

    def piece_of(r, n):
        return pl.ds(pl.multiple_of(r * ROWS + n * PIECE, PIECE), PIECE)

    def send_to(t, slot, chip, ns):
        for n in ns:
            for h in range(2):
                remote(inputs[t].at[pl.ds(n * PIECE, PIECE), lanes(h)], gathered.at[t, slot, piece_of(core, n)],
                       g_send.at[t, (slot * 2 + h) * PIECES + n], g_recv.at[t, (slot * 2 + core) * PIECES + n],
                       "blk", chip + h)

    def send_b(t, ns=range(PIECES)):
        send_to(t, 2, near_b[t], ns)

    def send_a(t, ns=range(PIECES)):
        send_to(t, 1, near_a[t], ns)

    def send_own(t):
        remote(inputs[t].at[:, lanes(other)], gathered.at[t, 0, rows(core)],
               g_send.at[t, 0], g_recv.at[t, 0], "blk", own + other)

    def arrived(dst, sem):
        pltpu.make_async_remote_copy(
            src_ref=dst, dst_ref=dst, send_sem=sem, recv_sem=sem,
            device_id={"blk": own + other}, device_id_type=MESH,
        ).wait_recv()

    def wait_own(t):
        local[t].wait()
        arrived(gathered.at[t, 0, rows(other)], g_recv.at[t, 0])

    def wait_slot(t, slot):
        for n in range(PIECES):
            for r in range(2):
                arrived(gathered.at[t, slot, piece_of(r, n)], g_recv.at[t, (slot * 2 + r) * PIECES + n])

    def wait_forward(t, ns=range(PIECES)):
        for n in ns:
            for r in range(2):
                arrived(gathered.at[t, 2, piece_of(r, n)], g_recv.at[t, (4 + r) * PIECES + n])
                remote(gathered.at[t, 2, piece_of(r, n)], gathered.at[t, 3, piece_of(r, n)],
                       g_send.at[t, (6 + r) * PIECES + n], g_recv.at[t, (6 + r) * PIECES + n], "blk", near_a[t] + core)

    key_z = (z, zka, zkb, zkab)
    down = lax.broadcasted_iota(jnp.int32, (SPAN, CHUNK), 0)

    def score_tile(j, i):
        s = dot(gathered[TK, j], gathered[TQ, i], NT)
        place = qpos[:, cols(i)]
        parts = []
        for n in range(4):
            first = order[4 * (x * 8 + key_z[j]) + n] * SPAN
            parts.append(jnp.where(down <= place - first, s[n * SPAN:(n + 1) * SPAN], LOW))
        s = jnp.concatenate(parts, axis=0)
        top = jnp.max(s, axis=0, keepdims=True)
        p = jnp.exp2((s - top) * SCALE2)
        chunk_sum[j:j + 1, cols(i)] = jnp.sum(p, axis=0, keepdims=True)
        chunk_max[j:j + 1, cols(i)] = top
        probs[j, :, cols(i)] = p.astype(BF16)

    def dprob_tile(j, i):
        dprobs[j, :, cols(i)] = dot(gathered[TV, j], gathered[TG, i], NT)

    for t in (TK, TQ, TG, TV):
        send_b(t)
    for t in (TK, TQ, TG, TV):
        send_a(t)
    for t in (TK, TQ, TG, TV):
        send_own(t)

    def scores(*tiles):
        for j, i in tiles:
            score_tile(j, i)

    wait_own(TK)
    wait_own(TQ)
    scores((0, 0))
    wait_slot(TQ, 1)
    scores((0, 1))
    wait_slot(TK, 1)
    scores((1, 0), (1, 1))
    wait_forward(TK)
    scores((2, 0), (2, 1))
    wait_forward(TQ)
    scores((0, 2), (1, 2), (2, 2))
    wait_slot(TK, 3)
    scores((3, 0), (3, 1), (3, 2))
    wait_slot(TQ, 3)
    scores((0, 3), (1, 3))
    wait_forward(TG)
    scores((2, 3), (3, 3))

    peers = (q_a, q_b, q_ab)
    tops = [chunk_max[j:j + 1, :] for j in range(4)]
    sums = [chunk_sum[j:j + 1, :] for j in range(4)]
    top = functools.reduce(jnp.maximum, tops)
    total = sum(s * jnp.exp2((m - top) * SCALE2) for s, m in zip(sums, tops))
    stat_out[0:1, :] = top
    stat_out[1:2, :] = total
    for n, peer in enumerate(peers):
        remote(stat_out, stat_in.at[n], s_send.at[n], s_recv.at[n], "blk", peer + core)

    def turned_row(ref_row, n):
        return jnp.concatenate([ref_row[:, cols(s ^ (n + 1))] for s in range(4)], axis=1)

    wait_forward(TV)
    wait_own(TV)
    wait_own(TG)
    wait_slot(TV, 1)
    wait_slot(TG, 1)
    for i in range(3):
        dprob_tile(0, i)
        dprob_tile(1, i)
    all_tops, all_sums = [top], [total]
    for n in range(3):
        arrived(stat_in.at[n], s_recv.at[n])
        all_tops.append(turned_row(stat_in.at[n, pl.ds(0, 1)], n))
        all_sums.append(turned_row(stat_in.at[n, pl.ds(1, 1)], n))
    whole_top = functools.reduce(jnp.maximum, all_tops)
    whole_sum = sum(s * jnp.exp2((m - whole_top) * SCALE2) for s, m in zip(all_sums, all_tops))
    inverse = 1.0 / whole_sum
    for j in range(4):
        factor[j:j + 1, :] = jnp.exp2((tops[j] - whole_top) * SCALE2) * inverse

    red_a = {RO: q_a, RQ: q_a, RK: k_a, RV: k_a}
    red_b = {RO: q_b, RQ: q_b, RK: k_b, RV: k_b}

    def reduce_ab(t, part, r):
        staged[t, 3, halves[r]] = part.astype(BF16)
        remote(staged.at[t, 3, halves[r]], from_a_mid.at[t, halves[r]],
               r_send.at[t, 6 + r], r_recv.at[t, 6 + r], "blk", red_a[t] + core)

    def reduce_b(t, held):
        for r in range(2):
            arrived(from_a_mid.at[t, halves[r]], r_recv.at[t, 6 + r])
            staged[t, 2, halves[r]] = (held[halves[r]] + from_a_mid[t, halves[r]].astype(F32)).astype(BF16)
            remote(staged.at[t, 2, halves[r]], from_b.at[t, core],
                   r_send.at[t, 1 + r], r_recv.at[t, 1 + core], "blk", red_b[t] + r)

    def reduce_straight(t, slot, part, chip, into, at_sem):
        staged[t, slot] = part.astype(BF16)
        for r in range(2):
            remote(staged.at[t, slot, halves[r]], into.at[t, core],
                   r_send.at[t, at_sem + r], r_recv.at[t, at_sem + core], "blk", chip + r)

    def reduce_a(t, part):
        reduce_straight(t, 1, part, red_a[t], from_a, 3)

    def reduce_own(t, part):
        staged[t, 0] = part.astype(BF16)
        remote(staged.at[t, 0, rows(other)], from_own.at[t, core],
               r_send.at[t, 5], r_recv.at[t, 5], "blk", own + other)
        from_own[t, core] = staged[t, 0, rows(core)]

    def reduced(t):
        arrived(from_own.at[t, other], r_recv.at[t, 5])
        for h in range(2):
            arrived(from_a.at[t, h], r_recv.at[t, 3 + h])
            arrived(from_b.at[t, h], r_recv.at[t, 1 + h])
        return [
            from_own[t, h].astype(F32) + from_a[t, h].astype(F32) + from_b[t, h].astype(F32)
            for h in range(2)
        ]

    def weigh_tile(j, i):
        p = probs[j, :, cols(i)] * factor[j:j + 1, cols(i)].astype(BF16)
        probs[j, :, cols(i)] = p
        return dot(gathered[TV, j].T, p, NN) if j < 3 else None

    for i in range(4):
        weigh_tile(3, i)
    wait_slot(TG, 3)

    def value_part(j):
        part = None
        for i in range(4):
            term = dot(probs[j, :, cols(i)], gathered[TG, i], NN)
            part = term if part is None else part + term
        return part

    part = value_part(3)
    for r in range(2):
        reduce_ab(RV, part[r * ROWS:(r + 1) * ROWS], r)
    for i in range(4):
        turned[:, cols(i)] = weigh_tile(0, i) + weigh_tile(1, i) + weigh_tile(2, i)
    reduce_a(RV, value_part(1))
    wait_slot(TV, 3)
    for i in range(4):
        o = turned[:, cols(i)] + dot(gathered[TV, 3].T, probs[3, :, cols(i)], NN)
        turned[:, cols(i)] = o
        delta_out[:, cols(i)] = jnp.sum(o * gathered[TG, i].astype(F32).T, axis=0, keepdims=True)
    for n, peer in enumerate(peers):
        remote(delta_out, delta_in.at[n], d_send.at[n], d_recv.at[n], "blk", peer + core)

    for i in (3, 2, 1, 0):
        o = turned[:, cols(i)].T
        if i == 3:
            reduce_straight(RO, 3, o, q_ab, from_ab, 6)
        elif i == 2:
            reduce_straight(RO, 2, o, q_b, from_b, 1)
        elif i == 1:
            reduce_a(RO, o)
        else:
            reduce_own(RO, o)
    value_held[...] = value_part(2)
    reduce_own(RV, value_part(0))

    for j, i in [(3, 0), (3, 1), (3, 2), (3, 3), (0, 3), (1, 3), (2, 3), (2, 0), (2, 1), (2, 2)]:
        dprob_tile(j, i)

    delta = delta_out[...]
    for n in range(3):
        arrived(delta_in.at[n], d_recv.at[n])
        delta = delta + turned_row(delta_in.at[n], n)
    delta_rows = [delta[:, i * CHUNK:(i + 1) * CHUNK] for i in range(4)]

    fresh_q = set()

    def grad_tile(j, i, part=pl.ds(0, CHUNK)):
        ds = (probs[j, part, cols(i)].astype(F32) * (dprobs[j, part, cols(i)] - delta_rows[i])).astype(BF16)
        query_part = dot(gathered[TK, j, part].T, ds, NN)
        if i in fresh_q:
            turned[:, cols(i)] += query_part
        else:
            turned[:, cols(i)] = query_part
        fresh_q.add(i)
        return dot(ds, gathered[TQ, i], NN)

    def query_part_of(i):
        return turned[:, cols(i)].T * SCALE

    for r in range(2):
        part = sum(grad_tile(3, i, halves[r]) for i in range(4))
        reduce_ab(RK, part * SCALE, r)
    for j in range(3):
        key_total[j] = grad_tile(j, 3)
    part = query_part_of(3)
    for r in range(2):
        reduce_ab(RQ, part[r * ROWS:(r + 1) * ROWS], r)
    key_held[...] = (key_total[2] + sum(grad_tile(2, i) for i in range(3))) * SCALE
    reduce_b(RV, value_held)
    for j in range(2):
        key_total[j] += grad_tile(j, 2)
    query_held[...] = query_part_of(2)
    reduce_a(RK, (key_total[1] + sum(grad_tile(1, i) for i in range(2))) * SCALE)
    reduce_own(RK, (key_total[0] + sum(grad_tile(0, i) for i in range(2))) * SCALE)
    reduce_a(RQ, query_part_of(1))
    reduce_own(RQ, query_part_of(0))
    def block_of(h):
        return pl.ds(pl.multiple_of(h * 2 * DH, 2 * DH), 2 * DH)

    mine = reduced(RO)
    for h in range(2):
        arrived(from_ab.at[RO, h], r_recv.at[RO, 6 + h])
    mine = [(mine[h] + from_ab[RO, h].astype(F32)).astype(BF16) for h in range(2)]
    att_out[:, block_of(head)] = jnp.concatenate(mine, axis=1)

    def piece_at(source, n):
        return pl.ds(pl.multiple_of(source * 2 * DH + n * DH, DH), DH)

    def share(source, base, targets, n):
        for m, target in enumerate(targets):
            remote(att_out.at[:, piece_at(source, n)], att_out.at[:, piece_at(source, n)],
                   h_send.at[2 * (base + m) + n], h_recv.at[2 * source + n], "head", target)

    def wait_share(source, n):
        arrived(att_out.at[:, piece_at(source, n)], h_recv.at[2 * source + n])

    for n in range(2):
        share(head, 0, [head_x] + heads_y, n)
    reduce_b(RK, key_held)
    reduce_b(RQ, query_held)

    def finish(t, out):
        part = reduced(t)
        for h in range(2):
            out[:, h * DH:(h + 1) * DH] = part[h].astype(BF16)

    finish(RV, dv_out)
    for n in range(2):
        wait_share(head_x, n)
        share(head_x, 4, heads_y, n)
    finish(RQ, dq_out)
    finish(RK, dk_out)
    for m in (1, 2, 3):
        for n in range(2):
            wait_share(xh * 4 + (y + m) % 4, n)
            wait_share((1 - xh) * 4 + (y + m) % 4, n)
    for copy in started:
        copy.wait_send()


def body(queries, key_vectors, value_vectors, out_grad, block_order):
    def flat(array):
        return array.reshape(ROWS, 2 * DH)

    vmem = pl.BlockSpec(memory_space=pltpu.VMEM)
    dma = pltpu.SemaphoreType.DMA
    small = jax.ShapeDtypeStruct((ROWS, 2 * DH), BF16)
    outs = pl.pallas_call(
        kernel,
        out_shape=(pltpu.VMEM((ROWS, 16 * DH), BF16),) + (pltpu.VMEM((ROWS, 2 * DH), BF16),) * 3,
        in_specs=[pl.BlockSpec(memory_space=pltpu.SMEM)] + [pl.BlockSpec(memory_space=pl.ANY)] * 4,
        out_specs=(vmem,) * 4,
        scratch_shapes=[
            pltpu.VMEM((4, 4, CHUNK, DH), BF16),
            pltpu.VMEM((4, CHUNK, WIDE), BF16),
            pltpu.VMEM((4, CHUNK, WIDE), F32),
            pltpu.VMEM((1, WIDE), jnp.int32),
            pltpu.VMEM((4, WIDE), F32),
            pltpu.VMEM((4, WIDE), F32),
            pltpu.VMEM((2, WIDE), F32),
            pltpu.VMEM((3, 2, WIDE), F32),
            pltpu.VMEM((1, WIDE), F32),
            pltpu.VMEM((3, 1, WIDE), F32),
            pltpu.VMEM((4, WIDE), F32),
            pltpu.VMEM((DH, WIDE), F32),
            pltpu.VMEM((4, CHUNK, DH), F32),
            pltpu.VMEM((CHUNK, DH), F32),
            pltpu.VMEM((CHUNK, DH), F32),
            pltpu.VMEM((CHUNK, DH), F32),
            pltpu.VMEM((4, 4, CHUNK, DH), BF16),
            pltpu.VMEM((4, CHUNK, DH), BF16),
            pltpu.VMEM((4, 2, ROWS, DH), BF16),
            pltpu.VMEM((4, 2, ROWS, DH), BF16),
            pltpu.VMEM((4, 2, ROWS, DH), BF16),
            pltpu.VMEM((1, 2, ROWS, DH), BF16),
            dma((4, 16)), dma((4, 16)),
            dma((4, 8)), dma((4, 8)),
            dma((3,)), dma((3,)),
            dma((3,)), dma((3,)),
            dma((14,)), dma((16,)),
        ],
        compiler_params=pltpu.CompilerParams(
            collective_id=0, has_side_effects=True, vmem_limit_bytes=56 << 20
        ),
        cost_estimate=pl.CostEstimate(
            flops=12 * WIDE * WIDE * DH, bytes_accessed=3 << 20, transcendentals=WIDE * WIDE
        ),
    )(block_order, flat(queries), flat(key_vectors), flat(value_vectors), flat(out_grad))
    attended, query_grad, key_grad, value_grad = outs
    return (
        attended.reshape(2, SPAN, 16 * DH),
        query_grad.reshape(2, SPAN, 2 * DH),
        key_grad.reshape(2, SPAN, 2 * DH),
        value_grad.reshape(2, SPAN, 2 * DH),
    )


def solution(mesh):
    split = P("blk", None, "head")
    return jax.shard_map(
        body,
        mesh=mesh,
        in_specs=(split, split, split, split, P()),
        out_specs=(P("blk", None, None), split, split, split),
        check_vma=False,
    )
```

```python
import functools
import math

import jax
import jax.numpy as jnp
from jax import lax
from jax.experimental import pallas as pl
from jax.experimental.pallas import tpu as pltpu
from jax.sharding import PartitionSpec as P

MESH = pl.DeviceIdType.MESH
DH = 128
SPAN = 128
ROWS = 256
CHUNK = 512
WIDE = 2048
SCALE = DH**-0.5
SCALE2 = DH**-0.5 * math.log2(math.e)
LOW = -1e30
F32 = jnp.float32
BF16 = jnp.bfloat16
NN = (((1,), (0,)), ((), ()))
NT = (((1,), (1,)), ((), ()))
TK, TQ, TV, TG = 0, 1, 2, 3
RO, RV, RK, RQ = 0, 1, 2, 3


def dot(a, b, dims):
    return lax.dot_general(a, b, dims, preferred_element_type=F32)


def kernel(
    order, q_in, k_in, v_in, g_in,
    att_out, dq_out, dk_out, dv_out,
    gathered, probs, dprobs, qpos, chunk_max, chunk_sum, stat_out, stat_in, delta_out, delta_in, factor,
    turned, key_total, value_held, key_held, query_held,
    staged, from_a_mid, from_a, from_b, from_own, from_ab,
    g_send, g_recv, r_send, r_recv, s_send, s_recv, d_send, d_recv, h_send, h_recv,
):
    blk = lax.axis_index("blk")
    head = lax.axis_index("head")
    core = blk % 2
    z = (blk // 2) % 8
    x = blk // 16
    odd = z % 2
    other = 1 - core
    y = head % 4
    xh = head // 4

    def at(xx, zz):
        return xx * 16 + zz * 2

    zq = z + 1 - 2 * odd
    zka = (z + 2 * odd + 7) % 8
    zkb = (z + 11 - 6 * odd) % 8
    zkab = (zkb + 2 * (1 - odd) + 7) % 8
    q_a, q_b, q_ab = at(1 - x, z), at(x, zq), at(1 - x, zq)
    k_a, k_b = at(x, zka), at(x, zkb)
    own = at(x, z)
    near_a = {TK: k_a, TV: k_a, TQ: q_a, TG: q_a}
    near_b = {TK: k_b, TV: k_b, TQ: q_b, TG: q_b}
    inputs = {TK: k_in, TV: v_in, TQ: q_in, TG: g_in}

    barrier = pltpu.get_barrier_semaphore()
    chips = (q_a, q_b, q_ab, k_a, k_b)
    for chip in chips:
        for r in range(2):
            pl.semaphore_signal(barrier, inc=1, device_id={"blk": chip + r}, device_id_type=MESH)
    pl.semaphore_signal(barrier, inc=1, device_id={"blk": own + other}, device_id_type=MESH)
    heads_y = [xh * 4 + (y + n) % 4 for n in (1, 2, 3)]
    head_x = (1 - xh) * 4 + y
    for target in heads_y + [head_x]:
        pl.semaphore_signal(barrier, inc=1, device_id={"head": target}, device_id_type=MESH)

    def lanes(h):
        return pl.ds(pl.multiple_of(h * DH, DH), DH)

    def rows(r):
        return pl.ds(pl.multiple_of(r * ROWS, ROWS), ROWS)

    def cols(i):
        return pl.ds(i * CHUNK, CHUNK)

    halves = (pl.ds(0, ROWS), pl.ds(ROWS, ROWS))

    local = {}
    for t in (TK, TQ, TV, TG):
        local[t] = pltpu.make_async_copy(
            inputs[t].at[:, lanes(core)], gathered.at[t, 0, rows(core)], g_recv.at[t, 1])
        local[t].start()
    lane = lax.broadcasted_iota(jnp.int32, (1, SPAN), 1)
    for s, (xx, zz) in enumerate(((x, z), (1 - x, z), (x, zq), (1 - x, zq))):
        for n in range(4):
            first = order[4 * (xx * 8 + zz) + n] * SPAN
            qpos[:, pl.ds(s * CHUNK + n * SPAN, SPAN)] = first + lane
    pl.semaphore_wait(barrier, 2 * len(chips) + 1 + 4)

    started = []

    def remote(src, dst, send, recv, axis, device):
        copy = pltpu.make_async_remote_copy(
            src_ref=src, dst_ref=dst, send_sem=send, recv_sem=recv,
            device_id={axis: device}, device_id_type=MESH,
        )
        copy.start()
        started.append(copy)

    PIECES = 1
    PIECE = ROWS // PIECES

    def piece_of(r, n):
        return pl.ds(pl.multiple_of(r * ROWS + n * PIECE, PIECE), PIECE)

    def send_to(t, slot, chip, hs, ns=range(PIECES)):
        for n in ns:
            for h in hs:
                remote(inputs[t].at[pl.ds(n * PIECE, PIECE), lanes(h)], gathered.at[t, slot, piece_of(core, n)],
                       g_send.at[t, (slot * 2 + h) * PIECES + n], g_recv.at[t, (slot * 2 + core) * PIECES + n],
                       "blk", chip + h)

    def send_b(t, h):
        send_to(t, 2, near_b[t], [h])

    def send_a(t, h):
        send_to(t, 1, near_a[t], [h])

    def send_own(t):
        remote(inputs[t].at[:, lanes(other)], gathered.at[t, 0, rows(core)],
               g_send.at[t, 0], g_recv.at[t, 0], "blk", own + other)

    def arrived(dst, sem):
        pltpu.make_async_remote_copy(
            src_ref=dst, dst_ref=dst, send_sem=sem, recv_sem=sem,
            device_id={"blk": own + other}, device_id_type=MESH,
        ).wait_recv()

    def wait_own(t):
        local[t].wait()
        arrived(gathered.at[t, 0, rows(other)], g_recv.at[t, 0])

    def wait_slot(t, slot):
        for n in range(PIECES):
            for r in range(2):
                arrived(gathered.at[t, slot, piece_of(r, n)], g_recv.at[t, (slot * 2 + r) * PIECES + n])

    def wait_forward(t, ns=range(PIECES)):
        for n in ns:
            for r in range(2):
                arrived(gathered.at[t, 2, piece_of(r, n)], g_recv.at[t, (4 + r) * PIECES + n])
                remote(gathered.at[t, 2, piece_of(r, n)], gathered.at[t, 3, piece_of(r, n)],
                       g_send.at[t, (6 + r) * PIECES + n], g_recv.at[t, (6 + r) * PIECES + n], "blk", near_a[t] + core)

    key_z = (z, zka, zkb, zkab)
    down = lax.broadcasted_iota(jnp.int32, (SPAN, CHUNK), 0)

    def score_tile(j, i):
        s = dot(gathered[TK, j], gathered[TQ, i], NT)
        place = qpos[:, cols(i)]
        parts = []
        for n in range(4):
            first = order[4 * (x * 8 + key_z[j]) + n] * SPAN
            parts.append(jnp.where(down <= place - first, s[n * SPAN:(n + 1) * SPAN], LOW))
        s = jnp.concatenate(parts, axis=0)
        top = jnp.max(s, axis=0, keepdims=True)
        p = jnp.exp2((s - top) * SCALE2)
        chunk_sum[j:j + 1, cols(i)] = jnp.sum(p, axis=0, keepdims=True)
        chunk_max[j:j + 1, cols(i)] = top
        probs[j, :, cols(i)] = p.astype(BF16)

    def dprob_tile(j, i):
        dprobs[j, :, cols(i)] = dot(gathered[TV, j], gathered[TG, i], NT)

    sequence = ((TK, 0), (TQ, 0), (TK, 1), (TQ, 1), (TG, 0), (TV, 0), (TG, 1), (TV, 1))
    for t, h in sequence:
        send_b(t, h)
    for t in (TK, TQ, TG, TV):
        send_own(t)
    for t, h in sequence:
        send_a(t, h)

    def scores(*tiles):
        for j, i in tiles:
            score_tile(j, i)

    wait_own(TK)
    wait_own(TQ)
    scores((0, 0))
    wait_slot(TQ, 1)
    scores((0, 1))
    wait_slot(TK, 1)
    scores((1, 0), (1, 1))
    wait_forward(TK)
    scores((2, 0), (2, 1))
    wait_forward(TQ)
    scores((0, 2), (1, 2), (2, 2))
    wait_slot(TK, 3)
    scores((3, 0), (3, 1), (3, 2))
    wait_slot(TQ, 3)
    scores((0, 3), (1, 3), (2, 3), (3, 3))

    peers = (q_a, q_b, q_ab)
    tops = [chunk_max[j:j + 1, :] for j in range(4)]
    sums = [chunk_sum[j:j + 1, :] for j in range(4)]
    top = functools.reduce(jnp.maximum, tops)
    total = sum(s * jnp.exp2((m - top) * SCALE2) for s, m in zip(sums, tops))
    stat_out[0:1, :] = top
    stat_out[1:2, :] = total
    for n, peer in enumerate(peers):
        remote(stat_out, stat_in.at[n], s_send.at[n], s_recv.at[n], "blk", peer + core)

    def turned_row(ref_row, n):
        return jnp.concatenate([ref_row[:, cols(s ^ (n + 1))] for s in range(4)], axis=1)

    wait_forward(TG)
    wait_forward(TV)
    wait_own(TV)
    wait_own(TG)
    wait_slot(TV, 1)
    wait_slot(TG, 1)
    for i in range(3):
        dprob_tile(0, i)
        dprob_tile(1, i)
    all_tops, all_sums = [top], [total]
    for n in range(3):
        arrived(stat_in.at[n], s_recv.at[n])
        all_tops.append(turned_row(stat_in.at[n, pl.ds(0, 1)], n))
        all_sums.append(turned_row(stat_in.at[n, pl.ds(1, 1)], n))
    whole_top = functools.reduce(jnp.maximum, all_tops)
    whole_sum = sum(s * jnp.exp2((m - whole_top) * SCALE2) for s, m in zip(all_sums, all_tops))
    inverse = 1.0 / whole_sum
    for j in range(4):
        factor[j:j + 1, :] = jnp.exp2((tops[j] - whole_top) * SCALE2) * inverse

    red_a = {RO: q_a, RQ: q_a, RK: k_a, RV: k_a}
    red_b = {RO: q_b, RQ: q_b, RK: k_b, RV: k_b}

    def reduce_ab(t, part, r):
        staged[t, 3, halves[r]] = part.astype(BF16)
        remote(staged.at[t, 3, halves[r]], from_a_mid.at[t, halves[r]],
               r_send.at[t, 6 + r], r_recv.at[t, 6 + r], "blk", red_a[t] + core)

    def reduce_b(t, held):
        for r in range(2):
            arrived(from_a_mid.at[t, halves[r]], r_recv.at[t, 6 + r])
            staged[t, 2, halves[r]] = (held[halves[r]] + from_a_mid[t, halves[r]].astype(F32)).astype(BF16)
            remote(staged.at[t, 2, halves[r]], from_b.at[t, core],
                   r_send.at[t, 1 + r], r_recv.at[t, 1 + core], "blk", red_b[t] + r)

    def reduce_straight(t, slot, part, chip, into, at_sem):
        staged[t, slot] = part.astype(BF16)
        for r in range(2):
            remote(staged.at[t, slot, halves[r]], into.at[t, core],
                   r_send.at[t, at_sem + r], r_recv.at[t, at_sem + core], "blk", chip + r)

    def reduce_a(t, part):
        reduce_straight(t, 1, part, red_a[t], from_a, 3)

    def reduce_own(t, part):
        staged[t, 0] = part.astype(BF16)
        remote(staged.at[t, 0, rows(other)], from_own.at[t, core],
               r_send.at[t, 5], r_recv.at[t, 5], "blk", own + other)
        from_own[t, core] = staged[t, 0, rows(core)]

    def reduced(t):
        arrived(from_own.at[t, other], r_recv.at[t, 5])
        for h in range(2):
            arrived(from_a.at[t, h], r_recv.at[t, 3 + h])
            arrived(from_b.at[t, h], r_recv.at[t, 1 + h])
        return [
            from_own[t, h].astype(F32) + from_a[t, h].astype(F32) + from_b[t, h].astype(F32)
            for h in range(2)
        ]

    def weigh_tile(j, i):
        p = probs[j, :, cols(i)] * factor[j:j + 1, cols(i)].astype(BF16)
        probs[j, :, cols(i)] = p
        return dot(gathered[TV, j].T, p, NN) if j < 3 else None

    def value_term(j, i):
        return dot(probs[j, :, cols(i)], gathered[TG, i], NN)

    for i in range(4):
        weigh_tile(3, i)
    for i in range(4):
        turned[:, cols(i)] = weigh_tile(0, i) + weigh_tile(1, i) + weigh_tile(2, i)
    for j in (3, 1, 2, 0):
        key_total[j] = value_term(j, 0) + value_term(j, 1) + value_term(j, 2)
    wait_slot(TG, 3)
    part = key_total[3] + value_term(3, 3)
    for r in range(2):
        reduce_ab(RV, part[r * ROWS:(r + 1) * ROWS], r)
    reduce_a(RV, key_total[1] + value_term(1, 3))
    wait_slot(TV, 3)
    for i in range(4):
        o = turned[:, cols(i)] + dot(gathered[TV, 3].T, probs[3, :, cols(i)], NN)
        turned[:, cols(i)] = o
        delta_out[:, cols(i)] = jnp.sum(o * gathered[TG, i].astype(F32).T, axis=0, keepdims=True)
    for n, peer in enumerate(peers):
        remote(delta_out, delta_in.at[n], d_send.at[n], d_recv.at[n], "blk", peer + core)
    for i in (3, 2, 1, 0):
        o = turned[:, cols(i)].T
        if i == 3:
            reduce_straight(RO, 3, o, q_ab, from_ab, 6)
        elif i == 2:
            reduce_straight(RO, 2, o, q_b, from_b, 1)
        elif i == 1:
            reduce_a(RO, o)
        else:
            reduce_own(RO, o)
    value_held[...] = key_total[2] + value_term(2, 3)
    reduce_own(RV, key_total[0] + value_term(0, 3))
    for j, i in [(3, 0), (3, 1), (3, 2), (3, 3), (0, 3), (1, 3), (2, 3), (2, 0), (2, 1), (2, 2)]:
        dprob_tile(j, i)

    delta = delta_out[...]
    for n in range(3):
        arrived(delta_in.at[n], d_recv.at[n])
        delta = delta + turned_row(delta_in.at[n], n)
    delta_rows = [delta[:, i * CHUNK:(i + 1) * CHUNK] for i in range(4)]

    def block_of(h):
        return pl.ds(pl.multiple_of(h * 2 * DH, 2 * DH), 2 * DH)

    def piece_at(source, n):
        return pl.ds(pl.multiple_of(source * 2 * DH + n * DH, DH), DH)

    near_y = [heads_y[0], heads_y[2]]
    far_y = heads_y[1]
    far_xy = (1 - xh) * 4 + (y + 2) % 4

    def share_copies(source, base, targets, n):
        return [
            pltpu.make_async_remote_copy(
                src_ref=att_out.at[:, piece_at(source, n)], dst_ref=att_out.at[:, piece_at(source, n)],
                send_sem=h_send.at[2 * (base + m) + n], recv_sem=h_recv.at[2 * source + n],
                device_id={"head": target}, device_id_type=MESH)
            for m, target in enumerate(targets)
        ]

    def share(source, base, targets, n):
        for copy in share_copies(source, base, targets, n):
            copy.start()

    def share_own():
        mine = reduced(RO)
        for h in range(2):
            arrived(from_ab.at[RO, h], r_recv.at[RO, 6 + h])
        mine = [(mine[h] + from_ab[RO, h].astype(F32)).astype(BF16) for h in range(2)]
        att_out[:, block_of(head)] = jnp.concatenate(mine, axis=1)
        for n in range(2):
            share(head, 0, [head_x, far_y] + near_y, n)

    fresh_q = set()

    def grad_tile(j, i, part=pl.ds(0, CHUNK)):
        ds = (probs[j, part, cols(i)].astype(F32) * (dprobs[j, part, cols(i)] - delta_rows[i])).astype(BF16)
        query_part = dot(gathered[TK, j, part].T, ds, NN)
        if i in fresh_q:
            turned[:, cols(i)] += query_part
        else:
            turned[:, cols(i)] = query_part
        fresh_q.add(i)
        return dot(ds, gathered[TQ, i], NN)

    def query_part_of(i):
        return turned[:, cols(i)].T * SCALE

    for r in range(2):
        part = sum(grad_tile(3, i, halves[r]) for i in range(4))
        reduce_ab(RK, part * SCALE, r)
    for j in range(3):
        key_total[j] = grad_tile(j, 3)
    part = query_part_of(3)
    for r in range(2):
        reduce_ab(RQ, part[r * ROWS:(r + 1) * ROWS], r)
    key_held[...] = (key_total[2] + sum(grad_tile(2, i) for i in range(3))) * SCALE
    reduce_b(RV, value_held)

    @pl.when(core == 1)
    def _():
        share_own()

    for j in range(2):
        key_total[j] += grad_tile(j, 2)
    query_held[...] = query_part_of(2)
    reduce_a(RK, (key_total[1] + sum(grad_tile(1, i) for i in range(2))) * SCALE)
    reduce_own(RK, (key_total[0] + sum(grad_tile(0, i) for i in range(2))) * SCALE)
    reduce_a(RQ, query_part_of(1))
    reduce_own(RQ, query_part_of(0))
    reduce_b(RK, key_held)
    reduce_b(RQ, query_held)

    @pl.when(core == 0)
    def _():
        share_own()


    def wait_share(source, n):
        arrived(att_out.at[:, piece_at(source, n)], h_recv.at[2 * source + n])

    def finish(t, out):
        part = reduced(t)
        for h in range(2):
            out[:, h * DH:(h + 1) * DH] = part[h].astype(BF16)

    finish(RV, dv_out)
    for n in range(2):
        wait_share(head_x, n)
        share(head_x, 4, near_y, n)
        wait_share(far_y, n)
        share(far_y, 6, [head_x], n)
    finish(RQ, dq_out)
    finish(RK, dk_out)
    for n in range(2):
        wait_share(far_xy, n)
        for m in (1, 3):
            wait_share(xh * 4 + (y + m) % 4, n)
            wait_share((1 - xh) * 4 + (y + m) % 4, n)
    for n in range(2):
        started.extend(share_copies(head, 0, [head_x, far_y] + near_y, n))
        started.extend(share_copies(head_x, 4, near_y, n))
        started.extend(share_copies(far_y, 6, [head_x], n))
    for copy in started:
        copy.wait_send()


def body(queries, key_vectors, value_vectors, out_grad, block_order):
    def flat(array):
        return array.reshape(ROWS, 2 * DH)

    vmem = pl.BlockSpec(memory_space=pltpu.VMEM)
    dma = pltpu.SemaphoreType.DMA
    small = jax.ShapeDtypeStruct((ROWS, 2 * DH), BF16)
    outs = pl.pallas_call(
        kernel,
        out_shape=(pltpu.VMEM((ROWS, 16 * DH), BF16),) + (pltpu.VMEM((ROWS, 2 * DH), BF16),) * 3,
        in_specs=[pl.BlockSpec(memory_space=pltpu.SMEM)] + [pl.BlockSpec(memory_space=pl.ANY)] * 4,
        out_specs=(vmem,) * 4,
        scratch_shapes=[
            pltpu.VMEM((4, 4, CHUNK, DH), BF16),
            pltpu.VMEM((4, CHUNK, WIDE), BF16),
            pltpu.VMEM((4, CHUNK, WIDE), F32),
            pltpu.VMEM((1, WIDE), jnp.int32),
            pltpu.VMEM((4, WIDE), F32),
            pltpu.VMEM((4, WIDE), F32),
            pltpu.VMEM((2, WIDE), F32),
            pltpu.VMEM((3, 2, WIDE), F32),
            pltpu.VMEM((1, WIDE), F32),
            pltpu.VMEM((3, 1, WIDE), F32),
            pltpu.VMEM((4, WIDE), F32),
            pltpu.VMEM((DH, WIDE), F32),
            pltpu.VMEM((4, CHUNK, DH), F32),
            pltpu.VMEM((CHUNK, DH), F32),
            pltpu.VMEM((CHUNK, DH), F32),
            pltpu.VMEM((CHUNK, DH), F32),
            pltpu.VMEM((4, 4, CHUNK, DH), BF16),
            pltpu.VMEM((4, CHUNK, DH), BF16),
            pltpu.VMEM((4, 2, ROWS, DH), BF16),
            pltpu.VMEM((4, 2, ROWS, DH), BF16),
            pltpu.VMEM((4, 2, ROWS, DH), BF16),
            pltpu.VMEM((1, 2, ROWS, DH), BF16),
            dma((4, 16)), dma((4, 16)),
            dma((4, 8)), dma((4, 8)),
            dma((3,)), dma((3,)),
            dma((3,)), dma((3,)),
            dma((14,)), dma((16,)),
        ],
        compiler_params=pltpu.CompilerParams(
            collective_id=0, has_side_effects=True, vmem_limit_bytes=56 << 20
        ),
        cost_estimate=pl.CostEstimate(
            flops=12 * WIDE * WIDE * DH, bytes_accessed=3 << 20, transcendentals=WIDE * WIDE
        ),
    )(block_order, flat(queries), flat(key_vectors), flat(value_vectors), flat(out_grad))
    attended, query_grad, key_grad, value_grad = outs
    return (
        attended.reshape(2, SPAN, 16 * DH),
        query_grad.reshape(2, SPAN, 2 * DH),
        key_grad.reshape(2, SPAN, 2 * DH),
        value_grad.reshape(2, SPAN, 2 * DH),
    )


def solution(mesh):
    split = P("blk", None, "head")
    return jax.shard_map(
        body,
        mesh=mesh,
        in_specs=(split, split, split, split, P()),
        out_specs=(P("blk", None, None), split, split, split),
        check_vma=False,
    )
```

```python
import functools
import math

import jax
import jax.numpy as jnp
from jax import lax
from jax.experimental import pallas as pl
from jax.experimental.pallas import tpu as pltpu
from jax.sharding import PartitionSpec as P

MESH = pl.DeviceIdType.MESH
DH = 128
SPAN = 128
ROWS = 256
CHUNK = 512
WIDE = 2048
SCALE = DH**-0.5
SCALE2 = DH**-0.5 * math.log2(math.e)
LOW = -1e30
F32 = jnp.float32
BF16 = jnp.bfloat16
NN = (((1,), (0,)), ((), ()))
NT = (((1,), (1,)), ((), ()))
TK, TQ, TV, TG = 0, 1, 2, 3
RO, RV, RK, RQ = 0, 1, 2, 3


def dot(a, b, dims):
    return lax.dot_general(a, b, dims, preferred_element_type=F32)


def kernel(
    order, q_in, k_in, v_in, g_in,
    att_out, dq_out, dk_out, dv_out,
    gathered, probs, dprobs, qpos, chunk_max, chunk_sum, stat_out, stat_in, delta_out, delta_in, factor,
    turned, key_total, value_held, key_held, query_held,
    staged, from_a_mid, from_a, from_b, from_own, from_ab,
    g_send, g_recv, r_send, r_recv, s_send, s_recv, d_send, d_recv, h_send, h_recv,
):
    blk = lax.axis_index("blk")
    head = lax.axis_index("head")
    core = blk % 2
    z = (blk // 2) % 8
    x = blk // 16
    odd = z % 2
    other = 1 - core
    y = head % 4
    xh = head // 4

    def at(xx, zz):
        return xx * 16 + zz * 2

    zq = z + 1 - 2 * odd
    zka = (z + 2 * odd + 7) % 8
    zkb = (z + 11 - 6 * odd) % 8
    zkab = (zkb + 2 * (1 - odd) + 7) % 8
    q_a, q_b, q_ab = at(1 - x, z), at(x, zq), at(1 - x, zq)
    k_a, k_b = at(x, zka), at(x, zkb)
    own = at(x, z)
    near_a = {TK: k_a, TV: k_a, TQ: q_a, TG: q_a}
    near_b = {TK: k_b, TV: k_b, TQ: q_b, TG: q_b}
    inputs = {TK: k_in, TV: v_in, TQ: q_in, TG: g_in}

    barrier = pltpu.get_barrier_semaphore()
    chips = (q_a, q_b, q_ab, k_a, k_b)
    for chip in chips:
        for r in range(2):
            pl.semaphore_signal(barrier, inc=1, device_id={"blk": chip + r}, device_id_type=MESH)
    pl.semaphore_signal(barrier, inc=1, device_id={"blk": own + other}, device_id_type=MESH)
    heads_y = [xh * 4 + (y + n) % 4 for n in (1, 2, 3)]
    head_x = (1 - xh) * 4 + y
    for target in heads_y + [head_x]:
        pl.semaphore_signal(barrier, inc=1, device_id={"head": target}, device_id_type=MESH)

    def lanes(h):
        return pl.ds(pl.multiple_of(h * DH, DH), DH)

    def rows(r):
        return pl.ds(pl.multiple_of(r * ROWS, ROWS), ROWS)

    def cols(i):
        return pl.ds(i * CHUNK, CHUNK)

    halves = (pl.ds(0, ROWS), pl.ds(ROWS, ROWS))

    local = {}
    for t in (TK, TQ, TV, TG):
        local[t] = pltpu.make_async_copy(
            inputs[t].at[:, lanes(core)], gathered.at[t, 0, rows(core)], g_recv.at[t, 1])
        local[t].start()
    lane = lax.broadcasted_iota(jnp.int32, (1, SPAN), 1)
    for s, (xx, zz) in enumerate(((x, z), (1 - x, z), (x, zq), (1 - x, zq))):
        for n in range(4):
            first = order[4 * (xx * 8 + zz) + n] * SPAN
            qpos[:, pl.ds(s * CHUNK + n * SPAN, SPAN)] = first + lane
    pl.semaphore_wait(barrier, 2 * len(chips) + 1 + 4)

    started = []

    def remote(src, dst, send, recv, axis, device):
        copy = pltpu.make_async_remote_copy(
            src_ref=src, dst_ref=dst, send_sem=send, recv_sem=recv,
            device_id={axis: device}, device_id_type=MESH,
        )
        copy.start()
        started.append(copy)

    PIECES = 1
    PIECE = ROWS // PIECES

    def piece_of(r, n):
        return pl.ds(pl.multiple_of(r * ROWS + n * PIECE, PIECE), PIECE)

    def send_to(t, slot, chip, hs, ns=range(PIECES)):
        for n in ns:
            for h in hs:
                remote(inputs[t].at[pl.ds(n * PIECE, PIECE), lanes(h)], gathered.at[t, slot, piece_of(core, n)],
                       g_send.at[t, (slot * 2 + h) * PIECES + n], g_recv.at[t, (slot * 2 + core) * PIECES + n],
                       "blk", chip + h)

    def send_b(t, h):
        send_to(t, 2, near_b[t], [h])

    def send_a(t, h):
        send_to(t, 1, near_a[t], [h])

    def send_own(t):
        remote(inputs[t].at[:, lanes(other)], gathered.at[t, 0, rows(core)],
               g_send.at[t, 0], g_recv.at[t, 0], "blk", own + other)

    def arrived(dst, sem):
        pltpu.make_async_remote_copy(
            src_ref=dst, dst_ref=dst, send_sem=sem, recv_sem=sem,
            device_id={"blk": own + other}, device_id_type=MESH,
        ).wait_recv()

    def wait_own(t):
        local[t].wait()
        arrived(gathered.at[t, 0, rows(other)], g_recv.at[t, 0])

    def wait_slot(t, slot):
        for n in range(PIECES):
            for r in range(2):
                arrived(gathered.at[t, slot, piece_of(r, n)], g_recv.at[t, (slot * 2 + r) * PIECES + n])

    def wait_forward(t, ns=range(PIECES)):
        for n in ns:
            for r in range(2):
                arrived(gathered.at[t, 2, piece_of(r, n)], g_recv.at[t, (4 + r) * PIECES + n])
                remote(gathered.at[t, 2, piece_of(r, n)], gathered.at[t, 3, piece_of(r, n)],
                       g_send.at[t, (6 + r) * PIECES + n], g_recv.at[t, (6 + r) * PIECES + n], "blk", near_a[t] + core)

    key_z = (z, zka, zkb, zkab)
    down = lax.broadcasted_iota(jnp.int32, (SPAN, CHUNK), 0)

    def score_tile(j, i):
        s = dot(gathered[TK, j], gathered[TQ, i], NT)
        place = qpos[:, cols(i)]
        parts = []
        for n in range(4):
            first = order[4 * (x * 8 + key_z[j]) + n] * SPAN
            parts.append(jnp.where(down <= place - first, s[n * SPAN:(n + 1) * SPAN], LOW))
        s = jnp.concatenate(parts, axis=0)
        top = jnp.max(s, axis=0, keepdims=True)
        p = jnp.exp2((s - top) * SCALE2)
        chunk_sum[j:j + 1, cols(i)] = jnp.sum(p, axis=0, keepdims=True)
        chunk_max[j:j + 1, cols(i)] = top
        probs[j, :, cols(i)] = p.astype(BF16)

    def dprob_tile(j, i):
        dprobs[j, :, cols(i)] = dot(gathered[TV, j], gathered[TG, i], NT)

    sequence = ((TK, 0), (TQ, 0), (TK, 1), (TQ, 1), (TG, 0), (TV, 0), (TG, 1), (TV, 1))
    for t, h in sequence:
        send_b(t, h)
    for t in (TK, TQ, TG, TV):
        send_own(t)
    for t, h in sequence:
        send_a(t, h)

    def scores(*tiles):
        for j, i in tiles:
            score_tile(j, i)

    wait_own(TK)
    wait_own(TQ)
    scores((0, 0))
    wait_slot(TQ, 1)
    scores((0, 1))
    wait_slot(TK, 1)
    scores((1, 0), (1, 1))
    wait_forward(TK)
    scores((2, 0), (2, 1))
    wait_forward(TQ)
    scores((0, 2), (1, 2), (2, 2))
    wait_slot(TK, 3)
    scores((3, 0), (3, 1), (3, 2))
    wait_slot(TQ, 3)
    scores((0, 3), (1, 3), (2, 3), (3, 3))

    peers = (q_a, q_b, q_ab)
    tops = [chunk_max[j:j + 1, :] for j in range(4)]
    sums = [chunk_sum[j:j + 1, :] for j in range(4)]
    top = functools.reduce(jnp.maximum, tops)
    total = sum(s * jnp.exp2((m - top) * SCALE2) for s, m in zip(sums, tops))
    stat_out[0:1, :] = top
    stat_out[1:2, :] = total
    for n, peer in enumerate(peers):
        remote(stat_out, stat_in.at[n], s_send.at[n], s_recv.at[n], "blk", peer + core)

    def turned_row(ref_row, n):
        return jnp.concatenate([ref_row[:, cols(s ^ (n + 1))] for s in range(4)], axis=1)

    wait_forward(TG)
    wait_forward(TV)
    wait_own(TV)
    wait_own(TG)
    wait_slot(TV, 1)
    wait_slot(TG, 1)
    for i in range(3):
        dprob_tile(0, i)
        dprob_tile(1, i)
    all_tops, all_sums = [top], [total]
    for n in range(3):
        arrived(stat_in.at[n], s_recv.at[n])
        all_tops.append(turned_row(stat_in.at[n, pl.ds(0, 1)], n))
        all_sums.append(turned_row(stat_in.at[n, pl.ds(1, 1)], n))
    whole_top = functools.reduce(jnp.maximum, all_tops)
    whole_sum = sum(s * jnp.exp2((m - whole_top) * SCALE2) for s, m in zip(all_sums, all_tops))
    inverse = 1.0 / whole_sum
    for j in range(4):
        factor[j:j + 1, :] = jnp.exp2((tops[j] - whole_top) * SCALE2) * inverse

    red_a = {RO: q_a, RQ: q_a, RK: k_a, RV: k_a}
    red_b = {RO: q_b, RQ: q_b, RK: k_b, RV: k_b}

    def reduce_ab(t, part, r):
        staged[t, 3, halves[r]] = part.astype(BF16)
        remote(staged.at[t, 3, halves[r]], from_a_mid.at[t, halves[r]],
               r_send.at[t, 6 + r], r_recv.at[t, 6 + r], "blk", red_a[t] + core)

    def reduce_b(t, held):
        for r in range(2):
            arrived(from_a_mid.at[t, halves[r]], r_recv.at[t, 6 + r])
            staged[t, 2, halves[r]] = (held[halves[r]] + from_a_mid[t, halves[r]].astype(F32)).astype(BF16)
            remote(staged.at[t, 2, halves[r]], from_b.at[t, core],
                   r_send.at[t, 1 + r], r_recv.at[t, 1 + core], "blk", red_b[t] + r)

    def reduce_straight(t, slot, part, chip, into, at_sem):
        staged[t, slot] = part.astype(BF16)
        for r in range(2):
            remote(staged.at[t, slot, halves[r]], into.at[t, core],
                   r_send.at[t, at_sem + r], r_recv.at[t, at_sem + core], "blk", chip + r)

    def reduce_a(t, part):
        reduce_straight(t, 1, part, red_a[t], from_a, 3)

    def reduce_own(t, part):
        staged[t, 0] = part.astype(BF16)
        remote(staged.at[t, 0, rows(other)], from_own.at[t, core],
               r_send.at[t, 5], r_recv.at[t, 5], "blk", own + other)
        from_own[t, core] = staged[t, 0, rows(core)]

    def reduced(t):
        arrived(from_own.at[t, other], r_recv.at[t, 5])
        for h in range(2):
            arrived(from_a.at[t, h], r_recv.at[t, 3 + h])
            arrived(from_b.at[t, h], r_recv.at[t, 1 + h])
        return [
            from_own[t, h].astype(F32) + from_a[t, h].astype(F32) + from_b[t, h].astype(F32)
            for h in range(2)
        ]

    def weigh_tile(j, i):
        p = probs[j, :, cols(i)] * factor[j:j + 1, cols(i)].astype(BF16)
        probs[j, :, cols(i)] = p
        return dot(gathered[TV, j].T, p, NN) if j < 3 else None

    def value_term(j, i):
        return dot(probs[j, :, cols(i)], gathered[TG, i], NN)

    for i in range(4):
        weigh_tile(3, i)
    for i in range(4):
        turned[:, cols(i)] = weigh_tile(0, i) + weigh_tile(1, i) + weigh_tile(2, i)
    for j in (3, 1, 2, 0):
        key_total[j] = value_term(j, 0) + value_term(j, 1) + value_term(j, 2)
    wait_slot(TG, 3)
    part = key_total[3] + value_term(3, 3)
    for r in range(2):
        reduce_ab(RV, part[r * ROWS:(r + 1) * ROWS], r)
    reduce_a(RV, key_total[1] + value_term(1, 3))
    wait_slot(TV, 3)
    for i in range(4):
        o = turned[:, cols(i)] + dot(gathered[TV, 3].T, probs[3, :, cols(i)], NN)
        turned[:, cols(i)] = o
        delta_out[:, cols(i)] = jnp.sum(o * gathered[TG, i].astype(F32).T, axis=0, keepdims=True)
    for n, peer in enumerate(peers):
        remote(delta_out, delta_in.at[n], d_send.at[n], d_recv.at[n], "blk", peer + core)
    for i in (3, 2, 1, 0):
        o = turned[:, cols(i)].T
        if i == 3:
            reduce_straight(RO, 3, o, q_ab, from_ab, 6)
        elif i == 2:
            reduce_straight(RO, 2, o, q_b, from_b, 1)
        elif i == 1:
            reduce_a(RO, o)
        else:
            reduce_own(RO, o)
    value_held[...] = key_total[2] + value_term(2, 3)
    reduce_own(RV, key_total[0] + value_term(0, 3))
    for j, i in [(3, 0), (3, 1), (3, 2), (3, 3), (0, 3), (1, 3), (2, 3), (2, 0), (2, 1), (2, 2)]:
        dprob_tile(j, i)

    delta = delta_out[...]
    for n in range(3):
        arrived(delta_in.at[n], d_recv.at[n])
        delta = delta + turned_row(delta_in.at[n], n)
    delta_rows = [delta[:, i * CHUNK:(i + 1) * CHUNK] for i in range(4)]

    def block_of(h):
        return pl.ds(pl.multiple_of(h * 2 * DH, 2 * DH), 2 * DH)

    def piece_at(source, n):
        return pl.ds(pl.multiple_of(source * 2 * DH + n * DH, DH), DH)

    near_y = [heads_y[0], heads_y[2]]
    far_y = heads_y[1]
    far_xy = (1 - xh) * 4 + (y + 2) % 4

    def share_copies(source, base, targets, n):
        return [
            pltpu.make_async_remote_copy(
                src_ref=att_out.at[:, piece_at(source, n)], dst_ref=att_out.at[:, piece_at(source, n)],
                send_sem=h_send.at[2 * (base + m) + n], recv_sem=h_recv.at[2 * source + n],
                device_id={"head": target}, device_id_type=MESH)
            for m, target in enumerate(targets)
        ]

    def share(source, base, targets, n):
        for copy in share_copies(source, base, targets, n):
            copy.start()

    def share_own():
        mine = reduced(RO)
        for h in range(2):
            arrived(from_ab.at[RO, h], r_recv.at[RO, 6 + h])
        mine = [(mine[h] + from_ab[RO, h].astype(F32)).astype(BF16) for h in range(2)]
        att_out[:, block_of(head)] = jnp.concatenate(mine, axis=1)
        for n in range(2):
            share(head, 0, [head_x, far_y] + near_y, n)

    fresh_q = set()

    def grad_tile(j, i, part=pl.ds(0, CHUNK)):
        ds = (probs[j, part, cols(i)].astype(F32) * (dprobs[j, part, cols(i)] - delta_rows[i])).astype(BF16)
        query_part = dot(gathered[TK, j, part].T, ds, NN)
        if i in fresh_q:
            turned[:, cols(i)] += query_part
        else:
            turned[:, cols(i)] = query_part
        fresh_q.add(i)
        return dot(ds, gathered[TQ, i], NN)

    def query_part_of(i):
        return turned[:, cols(i)].T * SCALE

    def first_key_tile(i, part):
        ds = (probs[3, part, cols(i)].astype(F32) * (dprobs[3, part, cols(i)] - delta_rows[i])).astype(BF16)
        probs[3, part, cols(i)] = ds
        return dot(ds, gathered[TQ, i], NN)

    def first_query_tile(i):
        turned[:, cols(i)] = dot(gathered[TK, 3].T, probs[3, :, cols(i)], NN)
        fresh_q.add(i)

    for r in range(2):
        part = sum(first_key_tile(i, halves[r]) for i in range(4))
        reduce_ab(RK, part * SCALE, r)
    first_query_tile(3)
    for j in range(3):
        key_total[j] = grad_tile(j, 3)
    part = query_part_of(3)
    for r in range(2):
        reduce_ab(RQ, part[r * ROWS:(r + 1) * ROWS], r)
    for i in range(3):
        first_query_tile(i)
    key_held[...] = (key_total[2] + sum(grad_tile(2, i) for i in range(3))) * SCALE
    reduce_b(RV, value_held)

    @pl.when(core == 1)
    def _():
        share_own()

    for j in range(2):
        key_total[j] += grad_tile(j, 2)
    query_held[...] = query_part_of(2)
    reduce_a(RK, (key_total[1] + sum(grad_tile(1, i) for i in range(2))) * SCALE)
    reduce_own(RK, (key_total[0] + sum(grad_tile(0, i) for i in range(2))) * SCALE)
    reduce_a(RQ, query_part_of(1))
    reduce_own(RQ, query_part_of(0))
    reduce_b(RK, key_held)
    reduce_b(RQ, query_held)

    @pl.when(core == 0)
    def _():
        share_own()


    def wait_share(source, n):
        arrived(att_out.at[:, piece_at(source, n)], h_recv.at[2 * source + n])

    def finish(t, out):
        part = reduced(t)
        for h in range(2):
            out[:, h * DH:(h + 1) * DH] = part[h].astype(BF16)

    finish(RV, dv_out)
    for n in range(2):
        wait_share(head_x, n)
        share(head_x, 4, near_y, n)
        wait_share(far_y, n)
        share(far_y, 6, [head_x], n)
    finish(RQ, dq_out)
    finish(RK, dk_out)
    for n in range(2):
        wait_share(far_xy, n)
        for m in (1, 3):
            wait_share(xh * 4 + (y + m) % 4, n)
            wait_share((1 - xh) * 4 + (y + m) % 4, n)
    for n in range(2):
        started.extend(share_copies(head, 0, [head_x, far_y] + near_y, n))
        started.extend(share_copies(head_x, 4, near_y, n))
        started.extend(share_copies(far_y, 6, [head_x], n))
    for copy in started:
        copy.wait_send()


def body(queries, key_vectors, value_vectors, out_grad, block_order):
    def flat(array):
        return array.reshape(ROWS, 2 * DH)

    vmem = pl.BlockSpec(memory_space=pltpu.VMEM)
    dma = pltpu.SemaphoreType.DMA
    small = jax.ShapeDtypeStruct((ROWS, 2 * DH), BF16)
    outs = pl.pallas_call(
        kernel,
        out_shape=(pltpu.VMEM((ROWS, 16 * DH), BF16),) + (pltpu.VMEM((ROWS, 2 * DH), BF16),) * 3,
        in_specs=[pl.BlockSpec(memory_space=pltpu.SMEM)] + [pl.BlockSpec(memory_space=pl.ANY)] * 4,
        out_specs=(vmem,) * 4,
        scratch_shapes=[
            pltpu.VMEM((4, 4, CHUNK, DH), BF16),
            pltpu.VMEM((4, CHUNK, WIDE), BF16),
            pltpu.VMEM((4, CHUNK, WIDE), F32),
            pltpu.VMEM((1, WIDE), jnp.int32),
            pltpu.VMEM((4, WIDE), F32),
            pltpu.VMEM((4, WIDE), F32),
            pltpu.VMEM((2, WIDE), F32),
            pltpu.VMEM((3, 2, WIDE), F32),
            pltpu.VMEM((1, WIDE), F32),
            pltpu.VMEM((3, 1, WIDE), F32),
            pltpu.VMEM((4, WIDE), F32),
            pltpu.VMEM((DH, WIDE), F32),
            pltpu.VMEM((4, CHUNK, DH), F32),
            pltpu.VMEM((CHUNK, DH), F32),
            pltpu.VMEM((CHUNK, DH), F32),
            pltpu.VMEM((CHUNK, DH), F32),
            pltpu.VMEM((4, 4, CHUNK, DH), BF16),
            pltpu.VMEM((4, CHUNK, DH), BF16),
            pltpu.VMEM((4, 2, ROWS, DH), BF16),
            pltpu.VMEM((4, 2, ROWS, DH), BF16),
            pltpu.VMEM((4, 2, ROWS, DH), BF16),
            pltpu.VMEM((1, 2, ROWS, DH), BF16),
            dma((4, 16)), dma((4, 16)),
            dma((4, 8)), dma((4, 8)),
            dma((3,)), dma((3,)),
            dma((3,)), dma((3,)),
            dma((14,)), dma((16,)),
        ],
        compiler_params=pltpu.CompilerParams(
            collective_id=0, has_side_effects=True, vmem_limit_bytes=56 << 20
        ),
        cost_estimate=pl.CostEstimate(
            flops=12 * WIDE * WIDE * DH, bytes_accessed=3 << 20, transcendentals=WIDE * WIDE
        ),
    )(block_order, flat(queries), flat(key_vectors), flat(value_vectors), flat(out_grad))
    attended, query_grad, key_grad, value_grad = outs
    return (
        attended.reshape(2, SPAN, 16 * DH),
        query_grad.reshape(2, SPAN, 2 * DH),
        key_grad.reshape(2, SPAN, 2 * DH),
        value_grad.reshape(2, SPAN, 2 * DH),
    )


def solution(mesh):
    split = P("blk", None, "head")
    return jax.shard_map(
        body,
        mesh=mesh,
        in_specs=(split, split, split, split, P()),
        out_specs=(P("blk", None, None), split, split, split),
        check_vma=False,
    )
```
